32 devices in a mesh: expert: 16 (over z, x, core), dp: 2 (over y).
Axes of the slice: x: 2, y: 2, z: 4, core: 2. Of those that a mesh axis runs over, the one named last changes fastest.
Arguments:
- tokens: bfloat16 [4096, 2048], P(('expert', 'dp')), may hold values from -6 to 6
- w_router: bfloat16 [2048, 16], replicated, may hold values from -0.125 to 0.125
- w_up: bfloat16 [16, 2048, 7168], P('expert', None, 'dp'), may hold values from -0.125 to 0.125
- w_down: bfloat16 [16, 7168, 2048], P('expert', 'dp'), may hold values from -0.0625 to 0.0625
- norm_gain: float32 [2048], replicated, may hold values from 0.25 to 1.75
- readout: bfloat16 [2048, 128], replicated, may hold values from -0.125 to 0.125
- expert_ids: int32 [4096, 2], P(('expert', 'dp')), may hold values from 0 to 15, all different within a row; in each aligned block of 128 rows (0 to 127, 128 to 255, ...) at most 16 rows name the same one
- substation_ids: int32 [4096], P(('expert', 'dp')), may hold values from 0 to 31
- hour_index: int32 [4096], P(('expert', 'dp')), may hold values from 0 to 7
- target: float32 [256, 128], replicated, may hold values from -24 to 24
Outputs:
- load_table: float32 [256, 128], P(('expert', 'dp'))
- loss_value: float32 [], replicated
- grad_down: bfloat16 [16, 7168, 2048], P('expert', 'dp')
The draws below stay inside these ranges and needn't reach their ends.
Inputs may be any that keep to these rules, and one draw needn't show every extreme that they name: `expert_ids`: each row names two different experts; among the 128 rows of one device every expert is named exactly 16 times.
All inputs are finite; a program needn't handle non-finite values.
Results may differ from the reference program's by a relative error of at most 0.0075.
Values may be sent and summed in bfloat16 or wider, within the bound.
A program may use at most 128 MiB of HBM per device.

```python
import math
import jax
import jax.numpy as jnp
import numpy as np
from jax import lax

D = 2048
FF = 7168
Q = 128
HOURS = 8
TOK_DEV = 128
EXPERTS = 16
CAP = 16
FD = 3584
TOKENS = 4096
KEYS = 256
SUBS = 32
N_EXPERT = 16
N_DP = 2


def touch_ends(array, rng, least, top_value):
    dims = array.shape
    spot = [jax.random.randint(jax.random.fold_in(rng, axis), (), 0, dims[axis]) for axis in range(len(dims))]
    array = array.at[tuple(spot)].set(least)
    longest = dims.index(max(dims))
    spot[longest] = (spot[longest] + 1) % dims[longest]
    return array.at[tuple(spot)].set(top_value)


def block_scale(key, extent, shards, smallest, high):
    factor_of = 1.0
    for dim, shards_of in shards:
        steps = jax.random.uniform(jax.random.fold_in(jax.random.fold_in(key, 6), dim), (shards_of,), jnp.float32, smallest / len(shards), high / len(shards))
        factor_of = factor_of * jnp.repeat(jnp.exp(steps), extent[dim] // shards_of).reshape((-1,) + (1,) * (len(extent) - 1 - dim))
    return factor_of


def deal_out(stream_key, own, number, rows, number_of, top, reach, slope):
    order = jax.random.permutation(stream_key, number_of)
    packed, ordinary = portions_of(number_of, rows * top, reach, slope, True), portions_of(number_of, rows * top, reach, slope, False)
    places = jnp.arange(number_of)

    def named(sizes, turn):
        used = int((sizes > 0).sum())
        fixed = max(1, used // 4)
        shifted = fixed + (places - fixed + turn * (used - fixed)) % max(1, number_of - fixed)
        return jnp.zeros((number_of,), jnp.int32).at[order[jnp.where(places < fixed, places, shifted)]].set(jnp.asarray(sizes, jnp.int32))

    sizes = jnp.where(number % 4 == 0, named(packed, number // 4), named(ordinary, number - number // 4 - 1))
    mixed = jax.random.permutation(jax.random.fold_in(own, 3), number_of)
    giver, taker = mixed[0:number_of // 2 * 2:2], mixed[1:number_of // 2 * 2:2]
    room = jnp.minimum(sizes[giver] - 1, reach - sizes[taker]) // 2
    room = jnp.where((giver == order[0]) | (taker == order[0]) | (sizes[taker] == 0), 0, jnp.maximum(room, 0))
    shifted = jax.random.randint(jax.random.fold_in(own, 4), (number_of // 2,), 0, 1 << 20) % (room + 1)
    sizes = sizes.at[giver].add(-shifted).at[taker].add(shifted)
    members = jnp.searchsorted(jnp.cumsum(sizes), jnp.arange(rows * top), side="right").astype(jnp.int32)
    grid = members.reshape(top, rows).T
    grid = grid[jax.random.permutation(jax.random.fold_in(own, 1), rows)]
    turn = jax.random.randint(jax.random.fold_in(own, 2), (rows, 1), 0, top)
    return jnp.take_along_axis(grid, (jnp.arange(top)[None, :] + turn) % top, axis=1)


def portions_of(amount, total, limit, skew, full):
    portions = [(1 << 20) // math.isqrt(standing ** skew) + 1 for standing in range(1, amount + 1)]
    largest = limit if full else min(limit, max(-(-total // amount), total * portions[0] // sum(portions)))
    least = 1 if total - largest >= amount - 1 else 0
    counts, rest = [largest] + [least] * (amount - 1), total - largest - least * (amount - 1)
    while rest > 0:
        movable = [i for i in range(1, amount) if counts[i] < largest] or [i for i in range(1, amount) if counts[i] < limit]
        pool, left = sum([portions[i] for i in movable]), rest
        for i in movable:
            extra = min(limit - counts[i], max(1, left * portions[i] // pool), rest)
            counts[i] = counts[i] + extra
            rest = rest - extra
    return np.array(counts)


def centred(own_key, extent, deviation, limit, cuts=(), kind=jnp.bfloat16):
    level = block_scale(own_key, extent, cuts, -0.22, 0.18) if cuts else 1.0
    entries = jax.random.normal(own_key, extent, jnp.float32) * deviation * level
    return jnp.minimum(jnp.maximum(entries, -limit), limit).astype(kind)


def setup_inputs(seed: int = 0) -> dict:
    key_of = jax.random.split(jax.random.key(seed), 11)
    tokens = centred(key_of[0], (TOKENS, D), 1.0, 6.0, ((0, 32),))
    w_router = centred(key_of[1], (D, EXPERTS), D ** -0.5, 0.125)
    w_up = centred(key_of[2], (EXPERTS, D, FF), D ** -0.5, 0.125, ((0, 16), (2, 2)))
    w_down = centred(key_of[3], (EXPERTS, FF, D), FF ** -0.5, 0.0625, ((0, 16), (1, 2)))
    norm_gain = jnp.clip(1.0 + 0.15 * jax.random.normal(key_of[4], (D,), jnp.float32), 0.25, 1.75)
    readout = centred(key_of[5], (D, Q), D ** -0.5, 0.125)
    expert_ids_keys = jax.random.split(jax.random.fold_in(key_of[6], 1), TOKENS // TOK_DEV)
    expert_ids_turns = jax.random.permutation(jax.random.fold_in(key_of[6], 3), TOKENS // TOK_DEV)
    expert_ids = jax.vmap(lambda own, number: deal_out(jax.random.fold_in(key_of[6], 2), own, number, TOK_DEV, EXPERTS, 2, CAP, 2))(expert_ids_keys, expert_ids_turns).reshape((TOKENS, 2))
    substation_ids = touch_ends(jax.random.randint(key_of[7], (TOKENS,), 0, SUBS), jax.random.fold_in(key_of[7], 1), 0, SUBS - 1).astype(jnp.int32)
    hour_index = touch_ends(jax.random.randint(key_of[8], (TOKENS,), 0, HOURS), jax.random.fold_in(key_of[8], 1), 0, HOURS - 1).astype(jnp.int32)
    target = centred(key_of[9], (KEYS, Q), 4.0, 24.0, (), jnp.float32)
    return {"tokens": tokens, "w_router": w_router, "w_up": w_up, "w_down": w_down, "norm_gain": norm_gain, "readout": readout, "expert_ids": expert_ids, "substation_ids": substation_ids, "hour_index": hour_index, "target": target}


def lift_rows(buffer_rows, up_matrix):
    return jax.nn.gelu(jnp.dot(buffer_rows, up_matrix, preferred_element_type=jnp.float32)).astype(jnp.bfloat16)

def reference(tokens, w_router, w_up, w_down, norm_gain, readout, expert_ids, substation_ids, hour_index, target):
    n_devices = N_EXPERT * N_DP
    flat_expert = expert_ids.reshape(-1).astype(jnp.int32)
    per_device = flat_expert.reshape(n_devices, 2 * TOK_DEV)
    one_hot = (per_device[:, :, None] == jnp.arange(EXPERTS, dtype=jnp.int32)[None, None, :]).astype(jnp.int32)
    position = lax.optimization_barrier(jnp.sum((jnp.cumsum(one_hot, axis=1) - 1) * one_hot, axis=2))
    device_row = jnp.arange(n_devices, dtype=jnp.int32)[:, None]
    flat_slot = (device_row * CAP + position).reshape(-1).astype(jnp.int32)
    depth = n_devices * CAP
    doubled = jnp.repeat(tokens, 2, axis=0)
    buffer = jnp.zeros((EXPERTS, depth, D), jnp.bfloat16).at[flat_expert, flat_slot].set(doubled)

    def forward(operands):
        buffer_rows, up_matrix, down_matrix = operands
        hidden = lift_rows(buffer_rows, up_matrix)
        parts = jnp.einsum('mdf,dfo->mdo', hidden.reshape(depth, N_DP, FD).astype(jnp.float32), down_matrix.reshape(N_DP, FD, D).astype(jnp.float32), precision=lax.Precision.HIGHEST)
        rounded = lax.optimization_barrier(parts.astype(jnp.bfloat16))
        return lax.optimization_barrier(jnp.sum(rounded.astype(jnp.float32), axis=1)).astype(jnp.bfloat16)
    expert_out = lax.map(forward, (buffer, w_up, w_down))
    per_token = expert_out[flat_expert, flat_slot].reshape(TOKENS, 2, D).astype(jnp.float32)
    logits = jnp.dot(tokens, w_router, preferred_element_type=jnp.float32)
    chosen = jnp.take_along_axis(logits, expert_ids.astype(jnp.int32), axis=1)
    gate_first = jax.nn.sigmoid(chosen[:, 0] - chosen[:, 1])
    gate_weights = jnp.stack([gate_first, 1.0 - gate_first], axis=1)
    mixed = tokens.astype(jnp.float32) + lax.optimization_barrier(jnp.sum(gate_weights[:, :, None] * per_token, axis=1))
    rscale = 1.0 / jnp.sqrt(lax.optimization_barrier(jnp.mean(mixed * mixed, axis=1, keepdims=True)) + 1e-05)
    normed = (mixed * rscale * norm_gain[None, :]).astype(jnp.bfloat16)
    loads = jnp.dot(normed, readout, preferred_element_type=jnp.float32)
    keys = (substation_ids * HOURS + hour_index).astype(jnp.int32)
    load_table = jax.ops.segment_sum(loads, keys, num_segments=KEYS)
    diff = load_table - target
    loss_value = 0.5 * jnp.mean(diff * diff)
    g_loads = diff[keys].astype(jnp.bfloat16)
    g_normed = jnp.dot(g_loads, readout.T, preferred_element_type=jnp.float32)
    scaled = g_normed * norm_gain[None, :]
    g_mixed = rscale * scaled - rscale ** 3 * mixed * lax.optimization_barrier(jnp.mean(scaled * mixed, axis=1, keepdims=True))
    g_assign = (gate_weights[:, :, None] * g_mixed[:, None, :]).astype(jnp.bfloat16).reshape(-1, D)
    g_buffer = jnp.zeros((EXPERTS, depth, D), jnp.bfloat16).at[flat_expert, flat_slot].set(g_assign)

    def backward(operands):
        buffer_rows, up_matrix, grad_rows = operands
        hidden = lift_rows(buffer_rows, up_matrix)
        return jnp.dot(hidden.T, grad_rows, preferred_element_type=jnp.float32).astype(jnp.bfloat16)
    grad_down = lax.map(backward, (buffer, w_up, g_buffer))
    return (load_table, loss_value, grad_down)
```

```python
import jax
import jax.numpy as jnp
from jax import lax
from jax.experimental import pallas as pl
from jax.experimental.pallas import tpu as pltpu
from jax.sharding import PartitionSpec as P

HOURS = 8
MESH = pl.DeviceIdType.MESH


def greet(n_expert, n_group):
    e, d = lax.axis_index("expert"), lax.axis_index("dp")
    barrier = pltpu.get_barrier_semaphore()

    @pl.loop(1, n_expert)
    def _(k):
        pl.semaphore_signal(
            barrier, inc=1, device_id=(lax.rem(e + k, n_expert), d), device_id_type=MESH
        )

    @pl.loop(1, n_group)
    def _(k):
        pl.semaphore_signal(
            barrier, inc=1, device_id=(e, lax.rem(d + k, n_group)), device_id_type=MESH
        )

    pl.semaphore_wait(barrier, n_expert + n_group - 2)


def dispatch_kernel(n_expert, n_group, src, out, own_sem, send_a, recv_a, send_b, recv_b):
    e, d = lax.axis_index("expert"), lax.axis_index("dp")
    greet(n_expert, n_group)

    def across(peer, row):
        return pltpu.make_async_remote_copy(
            src_ref=src.at[peer],
            dst_ref=out.at[d, row],
            send_sem=send_a.at[peer],
            recv_sem=recv_a.at[row],
            device_id=(peer, d),
            device_id_type=MESH,
        )

    def over(block, row, k):
        return pltpu.make_async_remote_copy(
            src_ref=block,
            dst_ref=out.at[d, row],
            send_sem=send_b.at[k, row],
            recv_sem=recv_b.at[k, row],
            device_id=(e, lax.rem(d + k, n_group)),
            device_id_type=MESH,
        )

    @pl.loop(1, n_expert)
    def _(k):
        across(lax.rem(e + k, n_expert), e).start()

    own = pltpu.make_async_copy(src.at[e], out.at[d, e], own_sem)
    own.start()
    for k in range(1, n_group):
        over(src.at[e], e, k).start()

    @pl.loop(1, n_expert)
    def _(k):
        row = lax.rem(e + n_expert - k, n_expert)
        across(row, row).wait_recv()
        for j in range(1, n_group):
            over(out.at[d, row], row, j).start()

    @pl.loop(0, n_expert)
    def _(k):
        row = lax.rem(e + n_expert - k, n_expert)
        for j in range(1, n_group):
            over(out.at[d, row], row, j).wait_send()
            came = lax.rem(d + n_group - j, n_group)
            pltpu.make_async_remote_copy(
                src_ref=out.at[came, row],
                dst_ref=out.at[came, row],
                send_sem=send_b.at[j, row],
                recv_sem=recv_b.at[j, row],
                device_id=(e, came),
                device_id_type=MESH,
            ).wait_recv()

    @pl.loop(1, n_expert)
    def _(k):
        across(lax.rem(e + k, n_expert), e).wait_send()

    own.wait()


def dispatch(blocks, n_group, collective_id):
    n_expert, capacity, width = blocks.shape
    return pl.pallas_call(
        lambda *refs: dispatch_kernel(n_expert, n_group, *refs),
        out_shape=jax.ShapeDtypeStruct((n_group, n_expert, capacity, width), blocks.dtype),
        in_specs=[pl.BlockSpec(memory_space=pl.ANY)],
        out_specs=pl.BlockSpec(memory_space=pl.ANY),
        scratch_shapes=[
            pltpu.SemaphoreType.DMA,
            pltpu.SemaphoreType.DMA((n_expert,)),
            pltpu.SemaphoreType.DMA((n_expert,)),
            pltpu.SemaphoreType.DMA((n_group, n_expert)),
            pltpu.SemaphoreType.DMA((n_group, n_expert)),
        ],
        compiler_params=pltpu.CompilerParams(collective_id=collective_id, has_side_effects=True),
        name="dispatch",
    )(blocks)


def collect_kernel(n_expert, n_group, part, out, held, summed, send_a, recv_a, send_b, recv_b):
    e, d = lax.axis_index("expert"), lax.axis_index("dp")
    greet(n_expert, n_group)

    def over(row, j):
        to = lax.rem(d + j, n_group)
        return pltpu.make_async_remote_copy(
            src_ref=part.at[to, row],
            dst_ref=held.at[j - 1, row],
            send_sem=send_b.at[j, row],
            recv_sem=recv_b.at[j, row],
            device_id=(e, to),
            device_id_type=MESH,
        )

    def across(peer, row):
        return pltpu.make_async_remote_copy(
            src_ref=summed.at[peer],
            dst_ref=out.at[row],
            send_sem=send_a.at[peer],
            recv_sem=recv_a.at[row],
            device_id=(peer, d),
            device_id_type=MESH,
        )

    def total(row):
        value = part[d, row].astype(jnp.float32)
        for j in range(1, n_group):
            over(row, j).wait_recv()
            value = value + held[j - 1, row].astype(jnp.float32)
        return value.astype(out.dtype)

    @pl.loop(1, n_expert + 1)
    def _(k):
        row = lax.rem(e + k, n_expert)
        for j in range(1, n_group):
            over(row, j).start()

    @pl.loop(1, n_expert)
    def _(k):
        row = lax.rem(e + k, n_expert)
        summed[row] = total(row)
        across(row, e).start()

    out[e] = total(e)

    @pl.loop(1, n_expert)
    def _(k):
        row = lax.rem(e + n_expert - k, n_expert)
        across(row, row).wait_recv()

    @pl.loop(1, n_expert)
    def _(k):
        across(lax.rem(e + k, n_expert), e).wait_send()

    @pl.loop(0, n_expert)
    def _(row):
        for j in range(1, n_group):
            over(row, j).wait_send()


def collect(parts, collective_id):
    n_group, n_expert, capacity, width = parts.shape
    return pl.pallas_call(
        lambda *refs: collect_kernel(n_expert, n_group, *refs),
        out_shape=jax.ShapeDtypeStruct((n_expert, capacity, width), parts.dtype),
        in_specs=[pl.BlockSpec(memory_space=pltpu.VMEM)],
        out_specs=pl.BlockSpec(memory_space=pltpu.VMEM),
        scratch_shapes=[
            pltpu.VMEM((max(n_group - 1, 1), n_expert, capacity, width), parts.dtype),
            pltpu.VMEM((n_expert, capacity, width), parts.dtype),
            pltpu.SemaphoreType.DMA((n_expert,)),
            pltpu.SemaphoreType.DMA((n_expert,)),
            pltpu.SemaphoreType.DMA((n_group, n_expert)),
            pltpu.SemaphoreType.DMA((n_group, n_expert)),
        ],
        compiler_params=pltpu.CompilerParams(
            collective_id=collective_id, has_side_effects=True, vmem_limit_bytes=40 * 2**20
        ),
        name="collect",
    )(parts)


def table_kernel(n_expert, n_group, part, target, own, diff, held, send_a, recv_a, send_b, recv_b):
    n = n_expert * n_group
    me = lax.axis_index("expert") * n_group + lax.axis_index("dp")

    def place(k):
        to = lax.rem(me + k, n)
        return to, (to // n_group, lax.rem(to, n_group))

    barrier = pltpu.get_barrier_semaphore()

    @pl.loop(1, n)
    def _(k):
        pl.semaphore_signal(barrier, inc=1, device_id=place(k)[1], device_id_type=MESH)

    pl.semaphore_wait(barrier, n - 1)

    @pl.loop(1, n)
    def _(k):
        to, device = place(k)
        pltpu.make_async_remote_copy(
            src_ref=part.at[to],
            dst_ref=held.at[me],
            send_sem=send_a,
            recv_sem=recv_a,
            device_id=device,
            device_id_type=MESH,
        ).start()

    held[me] = part[me]
    rest = pl.ds(0, n - 1)
    pltpu.make_async_copy(held.at[rest], held.at[rest], recv_a).wait()
    total = held[0]
    for i in range(1, n):
        total = total + held[i]
    own[...] = total
    diff[me] = total - target[me]

    @pl.loop(1, n)
    def _(k):
        _, device = place(k)
        pltpu.make_async_remote_copy(
            src_ref=diff.at[me],
            dst_ref=diff.at[me],
            send_sem=send_b,
            recv_sem=recv_b,
            device_id=device,
            device_id_type=MESH,
        ).start()

    pltpu.make_async_copy(part.at[rest], part.at[rest], send_a).wait()
    pltpu.make_async_copy(diff.at[rest], diff.at[rest], send_b).wait()
    pltpu.make_async_copy(diff.at[rest], diff.at[rest], recv_b).wait()


def table_sum(part, target, n_expert, n_group, collective_id):
    n = n_expert * n_group
    keys, channels = part.shape
    blocks = (n, keys // n, channels)
    own, diff = pl.pallas_call(
        lambda *refs: table_kernel(n_expert, n_group, *refs),
        out_shape=(
            jax.ShapeDtypeStruct(blocks[1:], part.dtype),
            jax.ShapeDtypeStruct(blocks, part.dtype),
        ),
        in_specs=[pl.BlockSpec(memory_space=pltpu.VMEM)] * 2,
        out_specs=[pl.BlockSpec(memory_space=pltpu.VMEM)] * 2,
        scratch_shapes=[pltpu.VMEM(blocks, part.dtype)] + [pltpu.SemaphoreType.DMA] * 4,
        compiler_params=pltpu.CompilerParams(collective_id=collective_id, has_side_effects=True),
        name="table",
    )(part.reshape(blocks), target.reshape(blocks))
    return own, diff.reshape(keys, channels)


def local(
    tokens,
    w_router,
    w_up,
    w_down,
    norm_gain,
    readout,
    expert_ids,
    substation_ids,
    hour_index,
    target,
):
    n_expert = lax.axis_size("expert")
    n_group = lax.axis_size("dp")
    tok_rows = tokens.shape[0]
    width = tokens.shape[1]
    capacity = 2 * tok_rows // n_expert
    slots_all = n_expert * capacity
    up_local = w_up[0]
    down_local = w_down[0]
    flat_expert = expert_ids.reshape(-1)
    one_hot = (flat_expert[:, None] == jnp.arange(n_expert, dtype=jnp.int32)[None, :]).astype(
        jnp.int32
    )
    order = jnp.arange(2 * tok_rows, dtype=jnp.int32)
    earlier = (order[None, :] < order[:, None]).astype(jnp.bfloat16)
    before = jnp.dot(earlier, one_hot.astype(jnp.bfloat16), preferred_element_type=jnp.float32)
    position = jnp.sum(before.astype(jnp.int32) * one_hot, axis=1)
    slot_index = flat_expert * capacity + position
    slot_hot = (slot_index[:, None] == jnp.arange(slots_all, dtype=jnp.int32)[None, :]).astype(
        jnp.float32
    )
    slot_pairs = slot_hot.reshape(tok_rows, 2, slots_all)
    placing = jnp.sum(slot_pairs, axis=1).astype(jnp.bfloat16)
    outgoing = lax.dot_general(
        placing, tokens, (((0,), (0,)), ((), ())), preferred_element_type=jnp.float32
    )
    outgoing = outgoing.astype(jnp.bfloat16).reshape(n_expert, capacity, width)
    logits = jnp.dot(tokens, w_router, preferred_element_type=jnp.float32)
    expert_hot = one_hot.reshape(tok_rows, 2, n_expert).astype(jnp.float32)
    chosen = jnp.sum(expert_hot * logits[:, None, :], axis=2)
    gate_first = jax.nn.sigmoid(chosen[:, 0] - chosen[:, 1])
    gate_weights = jnp.stack([gate_first, 1.0 - gate_first], axis=1)
    mixing = jnp.sum(gate_weights[:, :, None] * slot_pairs, axis=1)
    rows_all = n_group * slots_all
    arrived = dispatch(outgoing, n_group, 1).reshape(rows_all, width)
    hidden = jax.nn.gelu(jnp.dot(arrived, up_local, preferred_element_type=jnp.float32)).astype(
        jnp.bfloat16
    )
    parts = jnp.dot(hidden, down_local, preferred_element_type=jnp.float32).astype(jnp.bfloat16)
    returned = collect(parts.reshape(n_group, n_expert, capacity, width), 2)
    returned_rows = returned.reshape(slots_all, width).astype(jnp.float32)
    combined = jnp.dot(mixing, returned_rows, precision=lax.Precision.HIGHEST)
    mixed = tokens.astype(jnp.float32) + combined
    rscale = 1.0 / jnp.sqrt(jnp.mean(mixed * mixed, axis=1, keepdims=True) + 1e-05)
    normed = (mixed * rscale * norm_gain[None, :]).astype(jnp.bfloat16)
    loads = jnp.dot(normed, readout, preferred_element_type=jnp.float32)
    keys = substation_ids * HOURS + hour_index
    key_hot = (keys[None, :] == jnp.arange(target.shape[0], dtype=jnp.int32)[:, None]).astype(
        jnp.float32
    )
    partial_table = jnp.dot(key_hot, loads, precision=lax.Precision.HIGHEST)
    table_own, diff_all = table_sum(partial_table, target, n_expert, n_group, 3)
    loss_value = 0.5 * jnp.mean(diff_all * diff_all)
    g_loads = lax.dot_general(
        key_hot, diff_all, (((0,), (0,)), ((), ())), precision=lax.Precision.HIGHEST
    )
    g_loads = g_loads.astype(jnp.bfloat16)
    g_normed = lax.dot_general(
        g_loads, readout, (((1,), (1,)), ((), ())), preferred_element_type=jnp.float32
    )
    scaled = g_normed * norm_gain[None, :]
    g_mixed = rscale * scaled - rscale**3 * mixed * jnp.mean(scaled * mixed, axis=1, keepdims=True)
    g_slots = lax.dot_general(
        mixing, g_mixed, (((0,), (0,)), ((), ())), precision=lax.Precision.HIGHEST
    )
    g_slots = g_slots.astype(jnp.bfloat16).reshape(n_expert, capacity, width)
    g_arrived = dispatch(g_slots, n_group, 4).reshape(rows_all, width)
    grad_local = lax.dot_general(
        hidden,
        g_arrived,
        (((0,), (0,)), ((), ())),
        preferred_element_type=jnp.float32,
    )
    grad_down = grad_local.astype(jnp.bfloat16)[None, :, :]
    return (table_own, loss_value, grad_down)


def solution(mesh):
    placed = (
        P(("expert", "dp"), None),
        P(),
        P("expert", None, "dp"),
        P("expert", "dp", None),
        P(),
        P(),
        P(("expert", "dp"), None),
        P(("expert", "dp")),
        P(("expert", "dp")),
        P(),
    )
    return jax.shard_map(
        local,
        mesh=mesh,
        in_specs=placed,
        out_specs=(P(("expert", "dp"), None), P(), P("expert", "dp", None)),
        check_vma=False,
    )
```

```python
import jax
import jax.numpy as jnp
from jax import lax
from jax.experimental import pallas as pl
from jax.experimental.pallas import tpu as pltpu
from jax.sharding import PartitionSpec as P

HOURS = 8
MESH = pl.DeviceIdType.MESH


def greet(n_expert, n_group):
    e, d = lax.axis_index("expert"), lax.axis_index("dp")
    barrier = pltpu.get_barrier_semaphore()

    @pl.loop(1, n_expert)
    def _(k):
        pl.semaphore_signal(
            barrier, inc=1, device_id=(lax.rem(e + k, n_expert), d), device_id_type=MESH
        )

    @pl.loop(1, n_group)
    def _(k):
        pl.semaphore_signal(
            barrier, inc=1, device_id=(e, lax.rem(d + k, n_group)), device_id_type=MESH
        )

    pl.semaphore_wait(barrier, n_expert + n_group - 2)


class Rows:
    def __init__(self, n_expert, n_group, src, out, own_sem, send_a, recv_a, send_b, recv_b):
        self.n_expert, self.n_group = n_expert, n_group
        self.src, self.out = src, out
        self.send_a, self.recv_a, self.send_b, self.recv_b = send_a, recv_a, send_b, recv_b
        self.e, self.d = lax.axis_index("expert"), lax.axis_index("dp")
        self.own = pltpu.make_async_copy(src.at[self.e], out.at[self.d, self.e], own_sem)

    def across(self, peer, row):
        return pltpu.make_async_remote_copy(
            src_ref=self.src.at[peer],
            dst_ref=self.out.at[self.d, row],
            send_sem=self.send_a.at[peer],
            recv_sem=self.recv_a.at[row],
            device_id=(peer, self.d),
            device_id_type=MESH,
        )

    def over(self, block, row, k):
        return pltpu.make_async_remote_copy(
            src_ref=block,
            dst_ref=self.out.at[self.d, row],
            send_sem=self.send_b.at[k, row],
            recv_sem=self.recv_b.at[k, row],
            device_id=(self.e, lax.rem(self.d + k, self.n_group)),
            device_id_type=MESH,
        )

    def start(self):
        @pl.loop(1, self.n_expert)
        def _(k):
            self.across(lax.rem(self.e + k, self.n_expert), self.e).start()

        self.own.start()
        for k in range(1, self.n_group):
            self.over(self.src.at[self.e], self.e, k).start()

    def forward(self, first, last):
        @pl.loop(first, last)
        def _(k):
            row = lax.rem(self.e + self.n_expert - k, self.n_expert)
            self.across(row, row).wait_recv()
            for j in range(1, self.n_group):
                self.over(self.out.at[self.d, row], row, j).start()

    def finish(self):
        @pl.loop(0, self.n_expert)
        def _(k):
            row = lax.rem(self.e + self.n_expert - k, self.n_expert)
            for j in range(1, self.n_group):
                self.over(self.out.at[self.d, row], row, j).wait_send()
                came = lax.rem(self.d + self.n_group - j, self.n_group)
                pltpu.make_async_remote_copy(
                    src_ref=self.out.at[came, row],
                    dst_ref=self.out.at[came, row],
                    send_sem=self.send_b.at[j, row],
                    recv_sem=self.recv_b.at[j, row],
                    device_id=(self.e, came),
                    device_id_type=MESH,
                ).wait_recv()

        @pl.loop(1, self.n_expert)
        def _(k):
            self.across(lax.rem(self.e + k, self.n_expert), self.e).wait_send()

        self.own.wait()


def row_semaphores(n_expert, n_group):
    return [
        pltpu.SemaphoreType.DMA,
        pltpu.SemaphoreType.DMA((n_expert,)),
        pltpu.SemaphoreType.DMA((n_expert,)),
        pltpu.SemaphoreType.DMA((n_group, n_expert)),
        pltpu.SemaphoreType.DMA((n_group, n_expert)),
    ]


def dispatch_kernel(n_expert, n_group, *refs):
    rows = Rows(n_expert, n_group, *refs)
    greet(n_expert, n_group)
    rows.start()
    rows.forward(1, n_expert)
    rows.finish()


def dispatch(blocks, n_group, collective_id):
    n_expert, capacity, width = blocks.shape
    return pl.pallas_call(
        lambda *refs: dispatch_kernel(n_expert, n_group, *refs),
        out_shape=jax.ShapeDtypeStruct((n_group, n_expert, capacity, width), blocks.dtype),
        in_specs=[pl.BlockSpec(memory_space=pl.ANY)],
        out_specs=pl.BlockSpec(memory_space=pl.ANY),
        scratch_shapes=row_semaphores(n_expert, n_group),
        compiler_params=pltpu.CompilerParams(collective_id=collective_id, has_side_effects=True),
        name="dispatch",
    )(blocks)


def collect_kernel(n_expert, n_group, part, out, held, summed, send_a, recv_a, send_b, recv_b):
    e, d = lax.axis_index("expert"), lax.axis_index("dp")
    greet(n_expert, n_group)

    def over(row, j):
        to = lax.rem(d + j, n_group)
        return pltpu.make_async_remote_copy(
            src_ref=part.at[to, row],
            dst_ref=held.at[j - 1, row],
            send_sem=send_b.at[j, row],
            recv_sem=recv_b.at[j, row],
            device_id=(e, to),
            device_id_type=MESH,
        )

    def across(peer, row):
        return pltpu.make_async_remote_copy(
            src_ref=summed.at[peer],
            dst_ref=out.at[row],
            send_sem=send_a.at[peer],
            recv_sem=recv_a.at[row],
            device_id=(peer, d),
            device_id_type=MESH,
        )

    def total(row):
        value = part[d, row].astype(jnp.float32)
        for j in range(1, n_group):
            over(row, j).wait_recv()
            value = value + held[j - 1, row].astype(jnp.float32)
        return value.astype(out.dtype)

    @pl.loop(1, n_expert + 1)
    def _(k):
        row = lax.rem(e + k, n_expert)
        for j in range(1, n_group):
            over(row, j).start()

    @pl.loop(1, n_expert)
    def _(k):
        row = lax.rem(e + k, n_expert)
        summed[row] = total(row)
        across(row, e).start()

    out[e] = total(e)

    @pl.loop(1, n_expert)
    def _(k):
        row = lax.rem(e + n_expert - k, n_expert)
        across(row, row).wait_recv()

    @pl.loop(1, n_expert)
    def _(k):
        across(lax.rem(e + k, n_expert), e).wait_send()

    @pl.loop(0, n_expert)
    def _(row):
        for j in range(1, n_group):
            over(row, j).wait_send()


def collect(parts, collective_id):
    n_group, n_expert, capacity, width = parts.shape
    return pl.pallas_call(
        lambda *refs: collect_kernel(n_expert, n_group, *refs),
        out_shape=jax.ShapeDtypeStruct((n_expert, capacity, width), parts.dtype),
        in_specs=[pl.BlockSpec(memory_space=pltpu.VMEM)],
        out_specs=pl.BlockSpec(memory_space=pltpu.VMEM),
        scratch_shapes=[
            pltpu.VMEM((max(n_group - 1, 1), n_expert, capacity, width), parts.dtype),
            pltpu.VMEM((n_expert, capacity, width), parts.dtype),
            pltpu.SemaphoreType.DMA((n_expert,)),
            pltpu.SemaphoreType.DMA((n_expert,)),
            pltpu.SemaphoreType.DMA((n_group, n_expert)),
            pltpu.SemaphoreType.DMA((n_group, n_expert)),
        ],
        compiler_params=pltpu.CompilerParams(
            collective_id=collective_id, has_side_effects=True, vmem_limit_bytes=40 * 2**20
        ),
        name="collect",
    )(parts)


def exchange_kernel(
    n_expert,
    n_group,
    part,
    target,
    blocks,
    own,
    diff,
    out,
    held,
    send_a,
    recv_a,
    send_b,
    recv_b,
    *row_sems,
):
    rows = Rows(n_expert, n_group, blocks, out, *row_sems)
    n = n_expert * n_group
    me = lax.axis_index("expert") * n_group + lax.axis_index("dp")

    def place(k):
        to = lax.rem(me + k, n)
        return to, (to // n_group, lax.rem(to, n_group))

    barrier = pltpu.get_barrier_semaphore()

    @pl.loop(1, n)
    def _(k):
        pl.semaphore_signal(barrier, inc=1, device_id=place(k)[1], device_id_type=MESH)

    pl.semaphore_wait(barrier, n - 1)

    @pl.loop(1, n)
    def _(k):
        to, device = place(k)
        pltpu.make_async_remote_copy(
            src_ref=part.at[to],
            dst_ref=held.at[me],
            send_sem=send_a,
            recv_sem=recv_a,
            device_id=device,
            device_id_type=MESH,
        ).start()

    rows.start()
    early = 1 + n_expert // 4
    rows.forward(1, early)
    held[me] = part[me]
    rest = pl.ds(0, n - 1)
    pltpu.make_async_copy(held.at[rest], held.at[rest], recv_a).wait()
    total = held[0]
    for i in range(1, n):
        total = total + held[i]
    own[...] = total
    diff[me] = total - target[me]

    @pl.loop(1, n)
    def _(k):
        _, device = place(k)
        pltpu.make_async_remote_copy(
            src_ref=diff.at[me],
            dst_ref=diff.at[me],
            send_sem=send_b,
            recv_sem=recv_b,
            device_id=device,
            device_id_type=MESH,
        ).start()

    rows.forward(early, n_expert)
    rows.finish()
    pltpu.make_async_copy(part.at[rest], part.at[rest], send_a).wait()
    pltpu.make_async_copy(diff.at[rest], diff.at[rest], send_b).wait()
    pltpu.make_async_copy(diff.at[rest], diff.at[rest], recv_b).wait()


def exchange(part, target, rows, n_group, collective_id):
    n_expert, capacity, width = rows.shape
    n = n_expert * n_group
    keys, channels = part.shape
    blocks = (n, keys // n, channels)
    own, diff, out = pl.pallas_call(
        lambda *refs: exchange_kernel(n_expert, n_group, *refs),
        out_shape=(
            jax.ShapeDtypeStruct(blocks[1:], part.dtype),
            jax.ShapeDtypeStruct(blocks, part.dtype),
            jax.ShapeDtypeStruct((n_group, n_expert, capacity, width), rows.dtype),
        ),
        in_specs=[pl.BlockSpec(memory_space=pltpu.VMEM)] * 2 + [pl.BlockSpec(memory_space=pl.ANY)],
        out_specs=[pl.BlockSpec(memory_space=pltpu.VMEM)] * 2
        + [pl.BlockSpec(memory_space=pl.ANY)],
        scratch_shapes=[pltpu.VMEM(blocks, part.dtype)]
        + [pltpu.SemaphoreType.DMA] * 4
        + row_semaphores(n_expert, n_group),
        compiler_params=pltpu.CompilerParams(collective_id=collective_id, has_side_effects=True),
        name="exchange",
    )(part.reshape(blocks), target.reshape(blocks), rows)
    return own, diff.reshape(keys, channels), out


def halves(value):
    high = lax.reduce_precision(value, 8, 7)
    return [high.astype(jnp.bfloat16), (value - high).astype(jnp.bfloat16)]


def local(
    tokens,
    w_router,
    w_up,
    w_down,
    norm_gain,
    readout,
    expert_ids,
    substation_ids,
    hour_index,
    target,
):
    n_expert = lax.axis_size("expert")
    n_group = lax.axis_size("dp")
    tok_rows = tokens.shape[0]
    width = tokens.shape[1]
    capacity = 2 * tok_rows // n_expert
    slots_all = n_expert * capacity
    up_local = w_up[0]
    down_local = w_down[0]
    flat_expert = expert_ids.reshape(-1)
    one_hot = (flat_expert[:, None] == jnp.arange(n_expert, dtype=jnp.int32)[None, :]).astype(
        jnp.int32
    )
    order = jnp.arange(2 * tok_rows, dtype=jnp.int32)
    earlier = (order[None, :] < order[:, None]).astype(jnp.bfloat16)
    before = jnp.dot(earlier, one_hot.astype(jnp.bfloat16), preferred_element_type=jnp.float32)
    position = jnp.sum(before.astype(jnp.int32) * one_hot, axis=1)
    slot_index = flat_expert * capacity + position
    slot_hot = (slot_index[:, None] == jnp.arange(slots_all, dtype=jnp.int32)[None, :]).astype(
        jnp.float32
    )
    slot_pairs = slot_hot.reshape(tok_rows, 2, slots_all)
    placing = jnp.sum(slot_pairs, axis=1).astype(jnp.bfloat16)
    outgoing = lax.dot_general(
        placing, tokens, (((0,), (0,)), ((), ())), preferred_element_type=jnp.float32
    )
    outgoing = outgoing.astype(jnp.bfloat16).reshape(n_expert, capacity, width)
    logits = jnp.dot(tokens, w_router, preferred_element_type=jnp.float32)
    expert_hot = one_hot.reshape(tok_rows, 2, n_expert).astype(jnp.float32)
    chosen = jnp.sum(expert_hot * logits[:, None, :], axis=2)
    gate_first = jax.nn.sigmoid(chosen[:, 0] - chosen[:, 1])
    gate_weights = jnp.stack([gate_first, 1.0 - gate_first], axis=1)
    mixing = jnp.sum(gate_weights[:, :, None] * slot_pairs, axis=1)
    rows_all = n_group * slots_all
    arrived = dispatch(outgoing, n_group, 1).reshape(rows_all, width)
    hidden = jax.nn.gelu(jnp.dot(arrived, up_local, preferred_element_type=jnp.float32)).astype(
        jnp.bfloat16
    )
    parts = jnp.dot(hidden, down_local, preferred_element_type=jnp.float32).astype(jnp.bfloat16)
    returned = collect(parts.reshape(n_group, n_expert, capacity, width), 2)
    returned_rows = returned.reshape(slots_all, width).astype(jnp.float32)
    combined = jnp.dot(mixing, returned_rows, precision=lax.Precision.HIGHEST)
    mixed = tokens.astype(jnp.float32) + combined
    rscale = 1.0 / jnp.sqrt(jnp.mean(mixed * mixed, axis=1, keepdims=True) + 1e-05)
    normed = (mixed * rscale * norm_gain[None, :]).astype(jnp.bfloat16)
    loads = jnp.dot(normed, readout, preferred_element_type=jnp.float32)
    keys = substation_ids * HOURS + hour_index
    key_hot = (keys[None, :] == jnp.arange(target.shape[0], dtype=jnp.int32)[:, None]).astype(
        jnp.float32
    )
    partial_table = jnp.dot(key_hot, loads, precision=lax.Precision.HIGHEST)
    slots_of = jnp.sum(slot_pairs, axis=1)
    scale_slots = jnp.sum(slots_of * rscale, axis=0)
    gate_slots = jnp.sum(mixing, axis=0)
    key_slots = jnp.sum(slots_of * keys.astype(jnp.float32)[:, None], axis=0)
    columns = jnp.stack(
        halves(gate_slots * scale_slots) + halves(scale_slots * scale_slots) + halves(key_slots),
        axis=1,
    )
    lanes = 128
    columns = jnp.pad(columns, ((0, 0), (0, lanes - columns.shape[1])))
    mixed_slots = lax.dot_general(
        placing,
        mixed.astype(jnp.bfloat16),
        (((0,), (0,)), ((), ())),
        preferred_element_type=jnp.float32,
    ).astype(jnp.bfloat16)
    sent = jnp.concatenate([mixed_slots, columns], axis=1)
    table_own, diff_all, came = exchange(
        partial_table, target, sent.reshape(n_expert, capacity, width + lanes), n_group, 3
    )
    loss_value = 0.5 * jnp.mean(diff_all * diff_all)
    came = came.reshape(rows_all, width + lanes)
    mixed_came = came[:, :width].astype(jnp.float32)
    pairs = came[:, width:].astype(jnp.float32)
    gate_scale = pairs[:, 0:1] + pairs[:, 1:2]
    scale_squared = pairs[:, 2:3] + pairs[:, 3:4]
    key_came = (pairs[:, 4:5] + pairs[:, 5:6]).astype(jnp.int32)
    came_hot = (key_came == jnp.arange(target.shape[0], dtype=jnp.int32)[None, :]).astype(
        jnp.float32
    )
    g_loads = jnp.dot(came_hot, diff_all, precision=lax.Precision.HIGHEST).astype(jnp.bfloat16)
    g_normed = lax.dot_general(
        g_loads, readout, (((1,), (1,)), ((), ())), preferred_element_type=jnp.float32
    )
    scaled = g_normed * norm_gain[None, :]
    along = scale_squared * jnp.mean(scaled * mixed_came, axis=1, keepdims=True)
    g_arrived = (gate_scale * (scaled - mixed_came * along)).astype(jnp.bfloat16)
    grad_local = lax.dot_general(
        hidden,
        g_arrived,
        (((0,), (0,)), ((), ())),
        preferred_element_type=jnp.float32,
    )
    grad_down = grad_local.astype(jnp.bfloat16)[None, :, :]
    return (table_own, loss_value, grad_down)


def solution(mesh):
    placed = (
        P(("expert", "dp"), None),
        P(),
        P("expert", None, "dp"),
        P("expert", "dp", None),
        P(),
        P(),
        P(("expert", "dp"), None),
        P(("expert", "dp")),
        P(("expert", "dp")),
        P(),
    )
    return jax.shard_map(
        local,
        mesh=mesh,
        in_specs=placed,
        out_specs=(P(("expert", "dp"), None), P(), P("expert", "dp", None)),
        check_vma=False,
    )
```

```python
import jax
import jax.numpy as jnp
from jax import lax
from jax.experimental import pallas as pl
from jax.experimental.pallas import tpu as pltpu
from jax.sharding import PartitionSpec as P

HOURS = 8
MESH = pl.DeviceIdType.MESH


def partner(e, k, n, sign=1):
    if n & (n - 1):
        return lax.rem(e + n + sign * k, n)
    met, bit = 0, 1
    while bit < n:
        met = met + lax.rem(e // bit + k // bit, 2) * bit
        bit *= 2
    return met


def outward(e, k, n, sign=1):
    return lax.rem(e + n + sign * (n // 2 + (lax.rem(k, 2) * 2 - 1) * (k // 2)), n)


def greet(n_expert, n_group):
    e, d = lax.axis_index("expert"), lax.axis_index("dp")
    barrier = pltpu.get_barrier_semaphore()

    @pl.loop(1, n_expert)
    def _(k):
        pl.semaphore_signal(
            barrier, inc=1, device_id=(lax.rem(e + k, n_expert), d), device_id_type=MESH
        )

    @pl.loop(1, n_group)
    def _(k):
        pl.semaphore_signal(
            barrier, inc=1, device_id=(e, lax.rem(d + k, n_group)), device_id_type=MESH
        )

    pl.semaphore_wait(barrier, n_expert + n_group - 2)


class Rows:
    def __init__(self, n_expert, n_group, src, out, own_sem, send_a, recv_a, send_b, recv_b):
        self.n_expert, self.n_group = n_expert, n_group
        self.src, self.out = src, out
        self.send_a, self.recv_a, self.send_b, self.recv_b = send_a, recv_a, send_b, recv_b
        self.e, self.d = lax.axis_index("expert"), lax.axis_index("dp")
        self.own = pltpu.make_async_copy(src.at[self.e], out.at[self.d, self.e], own_sem)

    def across(self, peer, row):
        return pltpu.make_async_remote_copy(
            src_ref=self.src.at[peer],
            dst_ref=self.out.at[self.d, row],
            send_sem=self.send_a.at[peer],
            recv_sem=self.recv_a.at[row],
            device_id=(peer, self.d),
            device_id_type=MESH,
        )

    def over(self, block, row, k):
        return pltpu.make_async_remote_copy(
            src_ref=block,
            dst_ref=self.out.at[self.d, row],
            send_sem=self.send_b.at[k, row],
            recv_sem=self.recv_b.at[k, row],
            device_id=(self.e, lax.rem(self.d + k, self.n_group)),
            device_id_type=MESH,
        )

    def start(self):
        @pl.loop(1, self.n_expert)
        def _(k):
            self.across(partner(self.e, k, self.n_expert), self.e).start()

        self.own.start()
        for k in range(1, self.n_group):
            self.over(self.src.at[self.e], self.e, k).start()

    def forward(self, first, last):
        @pl.loop(first, last)
        def _(k):
            row = partner(self.e, k, self.n_expert, -1)
            self.across(row, row).wait_recv()
            for j in range(1, self.n_group):
                self.over(self.out.at[self.d, row], row, j).start()

    def finish(self):
        @pl.loop(0, self.n_expert)
        def _(k):
            row = partner(self.e, k, self.n_expert, -1)
            for j in range(1, self.n_group):
                self.over(self.out.at[self.d, row], row, j).wait_send()
                came = lax.rem(self.d + self.n_group - j, self.n_group)
                pltpu.make_async_remote_copy(
                    src_ref=self.out.at[came, row],
                    dst_ref=self.out.at[came, row],
                    send_sem=self.send_b.at[j, row],
                    recv_sem=self.recv_b.at[j, row],
                    device_id=(self.e, came),
                    device_id_type=MESH,
                ).wait_recv()

        @pl.loop(1, self.n_expert)
        def _(k):
            self.across(partner(self.e, k, self.n_expert), self.e).wait_send()

        self.own.wait()


def row_semaphores(n_expert, n_group):
    return [
        pltpu.SemaphoreType.DMA,
        pltpu.SemaphoreType.DMA((n_expert,)),
        pltpu.SemaphoreType.DMA((n_expert,)),
        pltpu.SemaphoreType.DMA((n_group, n_expert)),
        pltpu.SemaphoreType.DMA((n_group, n_expert)),
    ]


def dispatch_kernel(n_expert, n_group, *refs):
    rows = Rows(n_expert, n_group, *refs)
    greet(n_expert, n_group)
    rows.start()
    rows.forward(1, n_expert)
    rows.finish()


def dispatch(blocks, n_group, collective_id):
    n_expert, capacity, width = blocks.shape
    return pl.pallas_call(
        lambda *refs: dispatch_kernel(n_expert, n_group, *refs),
        out_shape=jax.ShapeDtypeStruct((n_group, n_expert, capacity, width), blocks.dtype),
        in_specs=[pl.BlockSpec(memory_space=pl.ANY)],
        out_specs=pl.BlockSpec(memory_space=pl.ANY),
        scratch_shapes=row_semaphores(n_expert, n_group),
        compiler_params=pltpu.CompilerParams(collective_id=collective_id, has_side_effects=True),
        name="dispatch",
    )(blocks)


def collect_kernel(n_expert, n_group, part, out, held, summed, send_a, recv_a, send_b, recv_b):
    e, d = lax.axis_index("expert"), lax.axis_index("dp")
    greet(n_expert, n_group)

    def over(row, j):
        to = lax.rem(d + j, n_group)
        return pltpu.make_async_remote_copy(
            src_ref=part.at[to, row],
            dst_ref=held.at[j - 1, row],
            send_sem=send_b.at[j, row],
            recv_sem=recv_b.at[j, row],
            device_id=(e, to),
            device_id_type=MESH,
        )

    def across(peer, row):
        return pltpu.make_async_remote_copy(
            src_ref=summed.at[peer],
            dst_ref=out.at[row],
            send_sem=send_a.at[peer],
            recv_sem=recv_a.at[row],
            device_id=(peer, d),
            device_id_type=MESH,
        )

    def total(row):
        value = part[d, row].astype(jnp.float32)
        for j in range(1, n_group):
            over(row, j).wait_recv()
            value = value + held[j - 1, row].astype(jnp.float32)
        return value.astype(out.dtype)

    @pl.loop(1, n_expert)
    def _(k):
        row = outward(e, k, n_expert)
        for j in range(1, n_group):
            over(row, j).start()

    for j in range(1, n_group):
        over(e, j).start()

    @pl.loop(1, n_expert)
    def _(k):
        row = outward(e, k, n_expert)
        summed[row] = total(row)
        across(row, e).start()

    out[e] = total(e)

    @pl.loop(1, n_expert)
    def _(k):
        row = outward(e, k, n_expert, -1)
        across(row, row).wait_recv()

    @pl.loop(1, n_expert)
    def _(k):
        across(outward(e, k, n_expert), e).wait_send()

    @pl.loop(0, n_expert)
    def _(row):
        for j in range(1, n_group):
            over(row, j).wait_send()


def collect(parts, collective_id):
    n_group, n_expert, capacity, width = parts.shape
    return pl.pallas_call(
        lambda *refs: collect_kernel(n_expert, n_group, *refs),
        out_shape=jax.ShapeDtypeStruct((n_expert, capacity, width), parts.dtype),
        in_specs=[pl.BlockSpec(memory_space=pltpu.VMEM)],
        out_specs=pl.BlockSpec(memory_space=pltpu.VMEM),
        scratch_shapes=[
            pltpu.VMEM((max(n_group - 1, 1), n_expert, capacity, width), parts.dtype),
            pltpu.VMEM((n_expert, capacity, width), parts.dtype),
            pltpu.SemaphoreType.DMA((n_expert,)),
            pltpu.SemaphoreType.DMA((n_expert,)),
            pltpu.SemaphoreType.DMA((n_group, n_expert)),
            pltpu.SemaphoreType.DMA((n_group, n_expert)),
        ],
        compiler_params=pltpu.CompilerParams(
            collective_id=collective_id, has_side_effects=True, vmem_limit_bytes=40 * 2**20
        ),
        name="collect",
    )(parts)


def exchange_kernel(
    n_expert,
    n_group,
    part,
    target,
    blocks,
    own,
    diff,
    out,
    held,
    send_a,
    recv_a,
    send_b,
    recv_b,
    *row_sems,
):
    rows = Rows(n_expert, n_group, blocks, out, *row_sems)
    n = n_expert * n_group
    me = lax.axis_index("expert") * n_group + lax.axis_index("dp")

    def place(k):
        to = lax.rem(me + k, n)
        return to, (to // n_group, lax.rem(to, n_group))

    barrier = pltpu.get_barrier_semaphore()

    @pl.loop(1, n)
    def _(k):
        pl.semaphore_signal(barrier, inc=1, device_id=place(k)[1], device_id_type=MESH)

    pl.semaphore_wait(barrier, n - 1)

    @pl.loop(1, n)
    def _(k):
        to, device = place(k)
        pltpu.make_async_remote_copy(
            src_ref=part.at[to],
            dst_ref=held.at[me],
            send_sem=send_a,
            recv_sem=recv_a,
            device_id=device,
            device_id_type=MESH,
        ).start()

    rows.start()
    early = 1 + n_expert // 4
    rows.forward(1, early)
    held[me] = part[me]
    rest = pl.ds(0, n - 1)
    pltpu.make_async_copy(held.at[rest], held.at[rest], recv_a).wait()
    total = held[0]
    for i in range(1, n):
        total = total + held[i]
    own[...] = total
    diff[me] = total - target[me]

    @pl.loop(1, n)
    def _(k):
        _, device = place(k)
        pltpu.make_async_remote_copy(
            src_ref=diff.at[me],
            dst_ref=diff.at[me],
            send_sem=send_b,
            recv_sem=recv_b,
            device_id=device,
            device_id_type=MESH,
        ).start()

    rows.forward(early, n_expert)
    rows.finish()
    pltpu.make_async_copy(part.at[rest], part.at[rest], send_a).wait()
    pltpu.make_async_copy(diff.at[rest], diff.at[rest], send_b).wait()
    pltpu.make_async_copy(diff.at[rest], diff.at[rest], recv_b).wait()


def exchange(part, target, rows, n_group, collective_id):
    n_expert, capacity, width = rows.shape
    n = n_expert * n_group
    keys, channels = part.shape
    blocks = (n, keys // n, channels)
    own, diff, out = pl.pallas_call(
        lambda *refs: exchange_kernel(n_expert, n_group, *refs),
        out_shape=(
            jax.ShapeDtypeStruct(blocks[1:], part.dtype),
            jax.ShapeDtypeStruct(blocks, part.dtype),
            jax.ShapeDtypeStruct((n_group, n_expert, capacity, width), rows.dtype),
        ),
        in_specs=[pl.BlockSpec(memory_space=pltpu.VMEM)] * 2 + [pl.BlockSpec(memory_space=pl.ANY)],
        out_specs=[pl.BlockSpec(memory_space=pltpu.VMEM)] * 2
        + [pl.BlockSpec(memory_space=pl.ANY)],
        scratch_shapes=[pltpu.VMEM(blocks, part.dtype)]
        + [pltpu.SemaphoreType.DMA] * 4
        + row_semaphores(n_expert, n_group),
        compiler_params=pltpu.CompilerParams(collective_id=collective_id, has_side_effects=True),
        name="exchange",
    )(part.reshape(blocks), target.reshape(blocks), rows)
    return own, diff.reshape(keys, channels), out


def halves(value):
    high = lax.reduce_precision(value, 8, 7)
    return [high.astype(jnp.bfloat16), (value - high).astype(jnp.bfloat16)]


def local(
    tokens,
    w_router,
    w_up,
    w_down,
    norm_gain,
    readout,
    expert_ids,
    substation_ids,
    hour_index,
    target,
):
    n_expert = lax.axis_size("expert")
    n_group = lax.axis_size("dp")
    tok_rows = tokens.shape[0]
    width = tokens.shape[1]
    capacity = 2 * tok_rows // n_expert
    slots_all = n_expert * capacity
    up_local = w_up[0]
    down_local = w_down[0]
    flat_expert = expert_ids.reshape(-1)
    one_hot = (flat_expert[:, None] == jnp.arange(n_expert, dtype=jnp.int32)[None, :]).astype(
        jnp.int32
    )
    order = jnp.arange(2 * tok_rows, dtype=jnp.int32)
    earlier = (order[None, :] < order[:, None]).astype(jnp.bfloat16)
    before = jnp.dot(earlier, one_hot.astype(jnp.bfloat16), preferred_element_type=jnp.float32)
    position = jnp.sum(before.astype(jnp.int32) * one_hot, axis=1)
    slot_index = flat_expert * capacity + position
    slot_hot = (slot_index[:, None] == jnp.arange(slots_all, dtype=jnp.int32)[None, :]).astype(
        jnp.float32
    )
    slot_pairs = slot_hot.reshape(tok_rows, 2, slots_all)
    placing = jnp.sum(slot_pairs, axis=1).astype(jnp.bfloat16)
    outgoing = lax.dot_general(
        placing, tokens, (((0,), (0,)), ((), ())), preferred_element_type=jnp.float32
    )
    outgoing = outgoing.astype(jnp.bfloat16).reshape(n_expert, capacity, width)
    logits = jnp.dot(tokens, w_router, preferred_element_type=jnp.float32)
    expert_hot = one_hot.reshape(tok_rows, 2, n_expert).astype(jnp.float32)
    chosen = jnp.sum(expert_hot * logits[:, None, :], axis=2)
    gate_first = jax.nn.sigmoid(chosen[:, 0] - chosen[:, 1])
    gate_weights = jnp.stack([gate_first, 1.0 - gate_first], axis=1)
    mixing = jnp.sum(gate_weights[:, :, None] * slot_pairs, axis=1)
    rows_all = n_group * slots_all
    arrived = dispatch(outgoing, n_group, 1).reshape(rows_all, width)
    hidden = jax.nn.gelu(jnp.dot(arrived, up_local, preferred_element_type=jnp.float32)).astype(
        jnp.bfloat16
    )
    parts = jnp.dot(hidden, down_local, preferred_element_type=jnp.float32).astype(jnp.bfloat16)
    returned = collect(parts.reshape(n_group, n_expert, capacity, width), 2)
    returned_rows = returned.reshape(slots_all, width).astype(jnp.float32)
    combined = jnp.dot(mixing, returned_rows, precision=lax.Precision.HIGHEST)
    mixed = tokens.astype(jnp.float32) + combined
    rscale = 1.0 / jnp.sqrt(jnp.mean(mixed * mixed, axis=1, keepdims=True) + 1e-05)
    normed = (mixed * rscale * norm_gain[None, :]).astype(jnp.bfloat16)
    loads = jnp.dot(normed, readout, preferred_element_type=jnp.float32)
    keys = substation_ids * HOURS + hour_index
    key_hot = (keys[None, :] == jnp.arange(target.shape[0], dtype=jnp.int32)[:, None]).astype(
        jnp.float32
    )
    partial_table = jnp.dot(key_hot, loads, precision=lax.Precision.HIGHEST)
    slots_of = jnp.sum(slot_pairs, axis=1)
    scale_slots = jnp.sum(slots_of * rscale, axis=0)
    gate_slots = jnp.sum(mixing, axis=0)
    key_slots = jnp.sum(slots_of * keys.astype(jnp.float32)[:, None], axis=0)
    columns = jnp.stack(
        halves(gate_slots * scale_slots) + halves(scale_slots * scale_slots) + halves(key_slots),
        axis=1,
    )
    lanes = 128
    columns = jnp.pad(columns, ((0, 0), (0, lanes - columns.shape[1])))
    mixed_slots = lax.dot_general(
        placing,
        mixed.astype(jnp.bfloat16),
        (((0,), (0,)), ((), ())),
        preferred_element_type=jnp.float32,
    ).astype(jnp.bfloat16)
    sent = jnp.concatenate([mixed_slots, columns], axis=1)
    table_own, diff_all, came = exchange(
        partial_table, target, sent.reshape(n_expert, capacity, width + lanes), n_group, 3
    )
    loss_value = 0.5 * jnp.mean(diff_all * diff_all)
    came = came.reshape(rows_all, width + lanes)
    mixed_came = came[:, :width].astype(jnp.float32)
    pairs = came[:, width:].astype(jnp.float32)
    gate_scale = pairs[:, 0:1] + pairs[:, 1:2]
    scale_squared = pairs[:, 2:3] + pairs[:, 3:4]
    key_came = (pairs[:, 4:5] + pairs[:, 5:6]).astype(jnp.int32)
    came_hot = (key_came == jnp.arange(target.shape[0], dtype=jnp.int32)[None, :]).astype(
        jnp.float32
    )
    g_loads = jnp.dot(came_hot, diff_all, precision=lax.Precision.HIGHEST).astype(jnp.bfloat16)
    g_normed = lax.dot_general(
        g_loads, readout, (((1,), (1,)), ((), ())), preferred_element_type=jnp.float32
    )
    scaled = g_normed * norm_gain[None, :]
    along = scale_squared * jnp.mean(scaled * mixed_came, axis=1, keepdims=True)
    g_arrived = (gate_scale * (scaled - mixed_came * along)).astype(jnp.bfloat16)
    grad_local = lax.dot_general(
        hidden,
        g_arrived,
        (((0,), (0,)), ((), ())),
        preferred_element_type=jnp.float32,
    )
    grad_down = grad_local.astype(jnp.bfloat16)[None, :, :]
    return (table_own, loss_value, grad_down)


def solution(mesh):
    placed = (
        P(("expert", "dp"), None),
        P(),
        P("expert", None, "dp"),
        P("expert", "dp", None),
        P(),
        P(),
        P(("expert", "dp"), None),
        P(("expert", "dp")),
        P(("expert", "dp")),
        P(),
    )
    return jax.shard_map(
        local,
        mesh=mesh,
        in_specs=placed,
        out_specs=(P(("expert", "dp"), None), P(), P("expert", "dp", None)),
        check_vma=False,
    )
```
